256 devices in a mesh: dp: 2 (over core), pb: 8 (over z_hi, x), ta: 16 (over z_lo, y).
Axes of the slice: x: 4, y: 4, z: 8 (z_hi: 2, z_lo: 4; z = z_hi * 4 + z_lo), core: 2. Of those that a mesh axis runs over, the one named last changes fastest.
Arguments:
- fmap1: bfloat16 [16384, 256], P(('dp', 'pb'), 'ta'), parts along dimension 0, may hold values from -6 to 6
- fmap2: bfloat16 [65536, 256], P(('dp', 'ta'), 'pb'), parts along dimension 0, may hold values from -6 to 6
- cot0: bfloat16 [16384, 32768], P(('dp', 'pb'), 'ta'), parts along dimension 0, may hold values from -0.75 to 0.75
- cot1: bfloat16 [16384, 8192], P(('dp', 'pb'), 'ta'), parts along dimension 0, may hold values from -3 to 3
- cot2: bfloat16 [16384, 2048], P(('dp', 'pb'), 'ta'), parts along dimension 0, may hold values from -6 to 6
- cot3: bfloat16 [16384, 512], P(('dp', 'pb'), 'ta'), parts along dimension 0, may hold values from -20 to 20
Outputs:
- corr0: bfloat16 [16384, 32768], P(('dp', 'pb'), 'ta'), parts along dimension 0
- corr1: bfloat16 [16384, 8192], P(('dp', 'pb'), 'ta'), parts along dimension 0
- corr2: bfloat16 [16384, 2048], P(('dp', 'pb'), 'ta'), parts along dimension 0
- corr3: bfloat16 [16384, 512], P(('dp', 'pb'), 'ta'), parts along dimension 0
- grad_query: bfloat16 [16384, 256], P(('dp', 'pb'), 'ta'), parts along dimension 0
- grad_target: bfloat16 [65536, 256], P(('dp', 'ta'), 'pb'), parts along dimension 0
The draws below stay inside these ranges and needn't reach their ends.
There are 2 independent parts, one for each index of `dp`. The reference program is written for one: setup_inputs(seed, part) draws one part's arguments, and reference() takes and returns one part's arrays. A program takes and returns all parts, laid end to end along the dimension named above; each array names one. Nothing has to cross between parts.
All inputs are finite; a program needn't handle non-finite values.
Results may differ from the reference program's by a relative error of at most 0.017.
Values may be sent and summed in bfloat16 or wider, within the bound.
A program may use at most 128 MiB of HBM per device.

```python
import math
import jax
import jax.numpy as jnp
from jax import lax

C = 256
W = 256
NQ = 8192
NT = 32768


def shard_levels(own_key, dims, cuts, low, largest):
    def one(axis_at, blocks):
        heights = jax.random.uniform(jax.random.fold_in(jax.random.fold_in(own_key, 6), axis_at), (blocks,), jnp.float32, low / len(cuts), largest / len(cuts))
        return jnp.repeat(jnp.exp(heights), dims[axis_at] // blocks).reshape((-1,) + (1,) * (len(dims) - axis_at - 1))

    gain = one(*cuts[0])
    for cut in cuts[1:]:
        gain = gain * one(*cut)
    return gain


def bell_draw(key, extent, width, bound, split=(), held_as=jnp.bfloat16):
    level = shard_levels(key, extent, split, -0.22, 0.18) if split else 1.0
    array = jax.random.normal(key, extent, jnp.float32) * width * level
    return jnp.minimum(jnp.maximum(array, -bound), bound).astype(held_as)


def setup_inputs(seed: int = 0, part: int = 0) -> dict:
    seeds = jax.random.split(jax.random.key(seed), 7)
    part_splits = jax.random.split(jax.random.fold_in(seeds[6], part), 7)
    return {
        "fmap1": bell_draw(part_splits[0], (NQ, C), 1.0, 6.0, ((0, 8), (1, 16))),
        "fmap2": bell_draw(part_splits[1], (NT, C), 1.0, 6.0, ((0, 16), (1, 8))),
        "cot0": bell_draw(part_splits[2], (NQ, NT), 0.05, 0.75, ((0, 8), (1, 16))),
        "cot1": bell_draw(part_splits[3], (NQ, NT // 4), 0.2, 3.0, ((0, 8), (1, 16))),
        "cot2": bell_draw(part_splits[4], (NQ, NT // 16), 0.8, 6.0, ((0, 8), (1, 16))),
        "cot3": bell_draw(part_splits[5], (NQ, NT // 64), 3.2, 20.0, ((0, 8), (1, 16))),
    }


def pool_last(volume, height, across):
    lead = volume.shape[:-1]
    shaped = volume.reshape(lead + (height // 2, 2, across // 2, 2))
    return lax.optimization_barrier(jnp.mean(shaped, axis=(-3, -1))).reshape(lead + (height * across // 4,))

def spread_last(coarse, height, across):
    lead = coarse.shape[:-1]
    shaped = coarse.reshape(lead + (height, 1, across, 1))
    shaped = jnp.broadcast_to(shaped, lead + (height, 2, across, 2))
    return 0.25 * shaped.reshape(lead + (height * across * 4,))

def combine_cotangents(first, second, third, fourth, height, across):
    merged = third.astype(jnp.float32) + spread_last(fourth.astype(jnp.float32), height // 8, across // 8)
    merged = second.astype(jnp.float32) + spread_last(merged, height // 4, across // 4)
    return first.astype(jnp.float32) + spread_last(merged, height // 2, across // 2)

def reference(fmap1, fmap2, cot0, cot1, cot2, cot3):
    factor = 1.0 / math.sqrt(C)
    height = NT // W
    stride = math.gcd(NQ, 256)
    blocks = NQ // stride

    def forward(query):
        volume = jnp.dot(query, fmap2.T, preferred_element_type=jnp.float32) * factor
        levels = [volume.astype(jnp.bfloat16)]
        rows_now = height
        cols_now = W
        for level in range(3):
            volume = pool_last(volume, rows_now, cols_now)
            rows_now = rows_now // 2
            cols_now = cols_now // 2
            levels.append(volume.astype(jnp.bfloat16))
        return tuple(levels)
    queries = fmap1.reshape(blocks, stride, C)
    pyramid = lax.map(forward, queries)

    def backward(total, pieces):
        query, first, second, third, fourth = pieces
        merged = combine_cotangents(first, second, third, fourth, height, W)
        weights = merged.astype(jnp.bfloat16)
        grad_rows = (jnp.dot(weights, fmap2, preferred_element_type=jnp.float32) * factor).astype(jnp.bfloat16)
        total = total + lax.dot_general(weights, query, (((0,), (0,)), ((), ())), preferred_element_type=jnp.float32)
        return (total, grad_rows)
    start = jnp.zeros((NT, C), jnp.float32)
    total, grads = lax.scan(backward, start, (queries, cot0.reshape(blocks, stride, NT), cot1.reshape(blocks, stride, NT // 4), cot2.reshape(blocks, stride, NT // 16), cot3.reshape(blocks, stride, NT // 64)))
    corr0 = pyramid[0].reshape(NQ, NT)
    corr1 = pyramid[1].reshape(NQ, NT // 4)
    corr2 = pyramid[2].reshape(NQ, NT // 16)
    corr3 = pyramid[3].reshape(NQ, NT // 64)
    return (corr0, corr1, corr2, corr3, grads.reshape(NQ, C), (total * factor).astype(jnp.bfloat16))
```

```python
import functools
import math

import jax
import jax.numpy as jnp
from jax import lax
from jax.experimental import pallas as pl
from jax.experimental.pallas import tpu as pltpu
from jax.sharding import PartitionSpec as P

C = 256
W = 256
MESH = pl.DeviceIdType.MESH
BF = jnp.bfloat16
F32 = jnp.float32
FACTOR = 1.0 / math.sqrt(C)


def mm(a, b, ca=1, cb=0):
    return lax.dot_general(a, b, (((ca,), (cb,)), ((), ())), preferred_element_type=F32)


def spread_matrix(rows, shift, value, offset=0):
    row = lax.broadcasted_iota(jnp.int32, (rows, W), 0) - offset
    col = lax.broadcasted_iota(jnp.int32, (rows, W), 1)
    return jnp.where(row == (col >> shift), value, 0.0)


def exchange(
    f1_ref, f2_ref, cot0_ref, cot1_ref, cot2_ref, cot3_ref,
    f1_full, f2_full, gt_sum, gt_in_z, gq_sum, gq_in_z,
    comb, c1, c2, c3, gt, gq, gt_in, gq_in, gt_out, gq_out,
    load_sem, own_sem, f1_send, f1_recv, f2_send, f2_recv, gt_send, gt_recv, gq_send, gq_recv,
):
    dp, pb, ta = lax.axis_index("dp"), lax.axis_index("pb"), lax.axis_index("ta")
    zh, x = pb // 4, pb % 4
    zl, y = ta // 4, ta % 4

    def at_x(k):
        return (dp, zh * 4 + (x + k) % 4, ta)

    def at_y(k):
        return (dp, pb, zl * 4 + (y + k) % 4)

    def at_zl(k):
        return (dp, pb, ((zl + k) % 4) * 4 + y)

    across = (dp, (1 - zh) * 4 + x, ta)

    def copy(src, dst, send, recv, to):
        return pltpu.make_async_remote_copy(
            src_ref=src, dst_ref=dst, send_sem=send, recv_sem=recv, device_id=to, device_id_type=MESH
        )

    loads = [
        pltpu.make_async_copy(src, dst, load_sem.at[i])
        for i, (src, dst) in enumerate(((cot3_ref, c3), (cot2_ref, c2), (cot1_ref, c1), (cot0_ref, comb)))
    ]
    own = [
        pltpu.make_async_copy(f1_ref, f1_full.at[zl, y], own_sem.at[0]),
        pltpu.make_async_copy(f2_ref, f2_full.at[pb], own_sem.at[1]),
    ]
    barrier = pltpu.get_barrier_semaphore()
    peers = [at_x(k) for k in (1, 2, 3)] + [at_y(k) for k in (1, 2, 3)] + [at_zl(k) for k in (1, 2, 3)] + [across]
    for peer in peers:
        pl.semaphore_signal(barrier, inc=1, device_id=peer, device_id_type=MESH)
    for c in own + loads:
        c.start()
    pl.semaphore_wait(barrier, len(peers))

    sent = []
    f1_z, f1_y, f2_x = [], [], []
    for k in (1, 2, 3):
        c = copy(f1_ref, f1_full.at[zl, y], f1_send.at[k - 1], f1_recv.at[k - 1], at_zl(k))
        c.start()
        sent.append(c)
        c = copy(f1_ref, f1_full.at[zl, y], f1_send.at[2 + k], f1_recv.at[2 + k], at_y(k))
        c.start()
        sent.append(c)
    f2_z = copy(f2_ref, f2_full.at[pb], f2_send.at[0], f2_recv.at[0], across)
    f2_z.start()
    sent.append(f2_z)
    for k in (1, 2, 3):
        c = copy(f2_ref, f2_full.at[pb], f2_send.at[k], f2_recv.at[k], at_x(k))
        c.start()
        sent.append(c)

    for k in (1, 2, 3):
        got = f1_full.at[(zl + 4 - k) % 4, y]
        copy(got, got, f1_send.at[k - 1], f1_recv.at[k - 1], at_zl(k)).wait_recv()
        for m in (1, 2, 3):
            i = 3 + 3 * k + m - 1
            c = copy(got, got, f1_send.at[i], f1_recv.at[i], at_y(m))
            c.start()
            sent.append(c)

    own[0].wait()
    own[1].wait()
    a3 = spread_matrix(32, 3, 1.0 / 64).astype(BF)
    fine = spread_matrix(128, 1, 0.25).astype(BF)
    coarse = [spread_matrix(128, 2, 1.0 / 16, 64 * j).astype(BF) for j in range(2)]
    both = [jnp.concatenate([fine, coarse[j]], axis=0) for j in range(2)]
    for c in loads:
        c.wait()

    def merge(i, _):
        rows = pl.ds(pl.multiple_of(i * 256, 256), 256)
        third = mm(c3[:, rows], a3, 0, 0)
        second = c2[rows, :]
        for k in range(4):
            left = jnp.concatenate([c1[rows, k * 128:(k + 1) * 128], second], axis=1)
            upper = mm(left, both[k // 2]) + third
            for r in (2 * k, 2 * k + 1):
                cols = slice(r * W, (r + 1) * W)
                comb[rows, cols] = (comb[rows, cols].astype(F32) + upper).astype(BF)
        return 0

    lax.fori_loop(0, comb.shape[0] // 256, merge, 0)

    other = f2_full.at[(1 - zh) * 4 + x]
    copy(other, other, f2_send.at[0], f2_recv.at[0], across).wait_recv()
    for k in (1, 2, 3):
        c = copy(other, other, f2_send.at[3 + k], f2_recv.at[3 + k], at_x(k))
        c.start()
        sent.append(c)

    for k in (1, 2, 3):
        block = f1_full.at[zl, (y + 4 - k) % 4]
        copy(block, block, f1_send.at[2 + k], f1_recv.at[2 + k], at_y(k)).wait_recv()
        for m in (1, 2, 3):
            i = 3 + 3 * m + k - 1
            block = f1_full.at[(zl + 4 - m) % 4, (y + 4 - k) % 4]
            copy(block, block, f1_send.at[i], f1_recv.at[i], at_y(k)).wait_recv()

    first = f1_full[...].reshape(C, comb.shape[0])

    def target(n, _):
        cols = pl.ds(pl.multiple_of(n * W, W), W)
        part = mm(first, comb[:, cols]) * FACTOR
        gt[:, :, :, cols] = part.astype(BF).reshape(2, 4, 32, W)
        return 0

    lax.fori_loop(0, comb.shape[1] // W, target, 0)
    for h in (0, 1):
        side = (1 - zh) if h == 0 else zh
        for k in (1, 2, 3):
            i = 3 * h + k - 1
            c = copy(gt.at[side, (x + k) % 4], gt_in.at[h, k - 1], gt_send.at[i], gt_recv.at[i], at_x(k))
            c.start()
            sent.append(c)

    for k in (1, 2, 3):
        block = f2_full.at[zh * 4 + (x + 4 - k) % 4]
        copy(block, block, f2_send.at[k], f2_recv.at[k], at_x(k)).wait_recv()
        block = f2_full.at[(1 - zh) * 4 + (x + 4 - k) % 4]
        copy(block, block, f2_send.at[3 + k], f2_recv.at[3 + k], at_x(k)).wait_recv()

    second = f2_full[...].reshape(C, comb.shape[1])

    def query(n, _):
        rows = pl.ds(pl.multiple_of(n * 256, 256), 256)
        part = mm(second, comb[rows, :], 1, 1) * FACTOR
        gq[:, :, :, rows] = part.astype(BF).reshape(4, 4, 16, 256)
        return 0

    lax.fori_loop(0, comb.shape[0] // 256, query, 0)
    for k in (1, 2, 3):
        c = copy(gq.at[:, (y + k) % 4], gq_in.at[k - 1], gq_send.at[k - 1], gq_recv.at[k - 1], at_y(k))
        c.start()
        sent.append(c)

    def gt_total(h, side):
        total = gt[side, x].astype(F32)
        for k in (1, 2, 3):
            i = 3 * h + k - 1
            copy(gt_in.at[h, k - 1], gt_in.at[h, k - 1], gt_send.at[i], gt_recv.at[i], at_x(k)).wait_recv()
            total = total + gt_in[h, k - 1].astype(F32)
        return total

    gt_out[...] = gt_total(0, 1 - zh).astype(BF)
    c = copy(gt_out, gt_in_z, gt_send.at[6], gt_recv.at[6], across)
    c.start()
    sent.append(c)

    for k in (1, 2, 3):
        copy(gq_in.at[k - 1], gq_in.at[k - 1], gq_send.at[k - 1], gq_recv.at[k - 1], at_y(k)).wait_recv()
    for k in (1, 2, 3, 0):
        to = (zl + k) % 4
        total = gq[to, y].astype(F32)
        for m in range(3):
            total = total + gq_in[m, to].astype(F32)
        if k:
            gq_out[k - 1] = total.astype(BF)
            c = copy(gq_out.at[k - 1], gq_in_z.at[k - 1], gq_send.at[2 + k], gq_recv.at[2 + k], at_zl(k))
            c.start()
            sent.append(c)
        else:
            gq_sum[...] = total
    gt_sum[...] = gt_total(1, zh)

    for k in (1, 2, 3):
        copy(gq_in_z.at[k - 1], gq_in_z.at[k - 1], gq_send.at[2 + k], gq_recv.at[2 + k], at_zl(k)).wait_recv()
    copy(gt_in_z, gt_in_z, gt_send.at[6], gt_recv.at[6], across).wait_recv()
    for c in sent:
        c.wait_send()


def volumes(
    f1_ref, f2_ref, gt_sum, gt_in_z, gq_sum, gq_in_z,
    corr0, corr1, corr2, corr3, grad_query, grad_target,
    p1, p2, p3,
):
    @pl.when(pl.program_id(0) == 0)
    def _():
        grad_target[...] = (gt_sum[...] + gt_in_z[...].astype(F32)).astype(BF)
        total = gq_sum[...]
        for k in range(3):
            total = total + gq_in_z[k].astype(F32)
        grad_query[...] = total.astype(BF)
        narrow = [spread_matrix(W // 2 ** l, l, 4.0 ** -l).astype(BF) for l in (1, 2, 3)]
        mean = jnp.concatenate(narrow + [jnp.zeros((32, W), BF)], axis=0)
        rows = [mm(f2_ref[:, r * W:(r + 1) * W], mean, 1, 1) for r in range(8)]
        pairs = [rows[2 * k] + rows[2 * k + 1] for k in range(4)]
        fours = [pairs[2 * k] + pairs[2 * k + 1] for k in range(2)]
        eight = fours[0] + fours[1]

        def put(ref, value, cols):
            high = value.astype(BF)
            ref[0, :, cols] = high
            ref[1, :, cols] = (value - high.astype(F32)).astype(BF)

        for k in range(4):
            put(p1, pairs[k][:, :128], slice(k * 128, (k + 1) * 128))
        put(p2, jnp.concatenate([f[:, 128:192] for f in fours], axis=1), slice(0, 128))
        put(p3, eight[:, 192:224], slice(0, 32))

    columns = f1_ref[...]
    query = columns.T
    corr0[...] = (mm(query, f2_ref[...]) * FACTOR).astype(BF)
    corr1[...] = ((mm(query, p1[0]) + mm(query, p1[1])) * FACTOR).astype(BF)
    corr2[...] = ((mm(query, p2[0]) + mm(query, p2[1])) * FACTOR).astype(BF)
    corr3[...] = ((mm(p3[0], columns, 0, 0) + mm(p3[1], columns, 0, 0)) * FACTOR).astype(BF)


def body(fmap1, fmap2, cot0, cot1, cot2, cot3):
    nq, nt = cot0.shape
    hbm = pl.BlockSpec(memory_space=pltpu.HBM)
    vmem = pl.BlockSpec(memory_space=pltpu.VMEM)
    dma = pltpu.SemaphoreType.DMA
    sds = jax.ShapeDtypeStruct
    f1_full, f2_full, gt_sum, gt_in_z, gq_sum, gq_in_z = pl.pallas_call(
        exchange,
        out_shape=(
            sds((4, 4, 16, nq), BF),
            sds((8, 32, nt), BF),
            sds((32, nt), F32),
            sds((32, nt), BF),
            sds((16, nq), F32),
            sds((3, 16, nq), BF),
        ),
        in_specs=[hbm] * 6,
        out_specs=(vmem,) * 6,
        scratch_shapes=[
            pltpu.VMEM((nq, nt), BF),
            pltpu.VMEM((nq, nt // 4), BF),
            pltpu.VMEM((nq, nt // 16), BF),
            pltpu.VMEM((nt // 64, nq), BF),
            pltpu.VMEM((2, 4, 32, nt), BF),
            pltpu.VMEM((4, 4, 16, nq), BF),
            pltpu.VMEM((2, 3, 32, nt), BF),
            pltpu.VMEM((3, 4, 16, nq), BF),
            pltpu.VMEM((32, nt), BF),
            pltpu.VMEM((3, 16, nq), BF),
            dma((4,)),
            dma((2,)),
            dma((15,)),
            dma((15,)),
            dma((7,)),
            dma((7,)),
            dma((7,)),
            dma((7,)),
            dma((6,)),
            dma((6,)),
        ],
        compiler_params=pltpu.CompilerParams(
            collective_id=0, has_side_effects=True, vmem_limit_bytes=40 * 2**20
        ),
        cost_estimate=pl.CostEstimate(flops=6 * nq * nt * C, bytes_accessed=16 * 2**20, transcendentals=0),
        name="exchange",
    )(*(pltpu.with_memory_space_constraint(a, pltpu.HBM) for a in (fmap1.T, fmap2.T, cot0, cot1, cot2, cot3.T)))

    block = 128
    whole = lambda *shape: pl.BlockSpec(shape, lambda i: (0,) * len(shape))
    corr0, corr1, corr2, corr3, grad_query, grad_target = pl.pallas_call(
        volumes,
        grid=(nq // block,),
        out_shape=(
            sds((nq, nt), BF),
            sds((nq, nt // 4), BF),
            sds((nq, nt // 16), BF),
            sds((nt // 64, nq), BF),
            sds((16, nq), BF),
            sds((32, nt), BF),
        ),
        in_specs=[
            pl.BlockSpec((C, block), lambda i: (0, i)),
            whole(C, nt),
            whole(32, nt),
            whole(32, nt),
            whole(16, nq),
            whole(3, 16, nq),
        ],
        out_specs=(
            pl.BlockSpec((block, nt), lambda i: (i, 0)),
            pl.BlockSpec((block, nt // 4), lambda i: (i, 0)),
            pl.BlockSpec((block, nt // 16), lambda i: (i, 0)),
            pl.BlockSpec((nt // 64, block), lambda i: (0, i)),
            whole(16, nq),
            whole(32, nt),
        ),
        scratch_shapes=[
            pltpu.VMEM((2, C, nt // 4), BF),
            pltpu.VMEM((2, C, nt // 16), BF),
            pltpu.VMEM((2, C, nt // 64), BF),
        ],
        compiler_params=pltpu.CompilerParams(vmem_limit_bytes=40 * 2**20),
        cost_estimate=pl.CostEstimate(flops=4 * nq * nt * C, bytes_accessed=8 * 2**20, transcendentals=0),
        name="volumes",
    )(f1_full.reshape(C, nq), f2_full.reshape(C, nt), gt_sum, gt_in_z, gq_sum, gq_in_z)
    return corr0, corr1, corr2, corr3.T, grad_query.T, grad_target.T


def solution(mesh):
    rows, flat = P(("dp", "pb"), "ta"), P(("dp", "ta"), "pb")
    return jax.shard_map(
        body,
        mesh=mesh,
        in_specs=(rows, flat, rows, rows, rows, rows),
        out_specs=(rows, rows, rows, rows, rows, flat),
        check_vma=False,
    )
```

```python
import functools
import math

import jax
import jax.numpy as jnp
from jax import lax
from jax.experimental import pallas as pl
from jax.experimental.pallas import tpu as pltpu
from jax.sharding import PartitionSpec as P

C = 256
W = 256
MESH = pl.DeviceIdType.MESH
BF = jnp.bfloat16
F32 = jnp.float32
FACTOR = 1.0 / math.sqrt(C)


def mm(a, b, ca=1, cb=0):
    return lax.dot_general(a, b, (((ca,), (cb,)), ((), ())), preferred_element_type=F32)


def spread_matrix(rows, shift, value, offset=0):
    row = lax.broadcasted_iota(jnp.int32, (rows, W), 0) - offset
    col = lax.broadcasted_iota(jnp.int32, (rows, W), 1)
    return jnp.where(row == (col >> shift), value, 0.0)


def exchange(
    f1_ref, f2_ref, cot0_ref, cot1_ref, cot2_ref, cot3_ref,
    corr0, corr1, corr2, corr3, gt_sum, gt_in_z, gq_sum, gq_in_z,
    f1_full, f2_full, comb, c1, c2, c3, p1, p2, p3, gt, gq, gt_in, gt_mid, gt_out, gq_in, gq_out,
    load_sem, own_sem, f1_send, f1_recv, f2_send, f2_recv, gt_send, gt_recv, gq_send, gq_recv,
):
    dp, pb, ta = lax.axis_index("dp"), lax.axis_index("pb"), lax.axis_index("ta")
    zh, x = pb // 4, pb % 4
    zl, y = ta // 4, ta % 4
    nq, nt = comb.shape
    halves = (pl.ds(0, 16), pl.ds(16, 16))

    def near(k):
        return (x + k) % 4

    def at_x(k):
        return (dp, zh * 4 + near(k), ta)

    def at_y(k):
        return (dp, pb, zl * 4 + (y + k) % 4)

    def at_zl(k):
        return (dp, pb, ((zl + k) % 4) * 4 + y)

    across = (dp, (1 - zh) * 4 + x, ta)

    def copy(src, dst, send, recv, to):
        return pltpu.make_async_remote_copy(
            src_ref=src, dst_ref=dst, send_sem=send, recv_sem=recv, device_id=to, device_id_type=MESH
        )

    sent = []

    def start(*args):
        c = copy(*args)
        c.start()
        sent.append(c)

    def arrived(dst, send, recv, to):
        copy(dst, dst, send, recv, to).wait_recv()

    loads = [
        pltpu.make_async_copy(src, dst, load_sem.at[i])
        for i, (src, dst) in enumerate(((cot3_ref, c3), (cot2_ref, c2), (cot1_ref, c1), (cot0_ref, comb)))
    ]
    own = [
        pltpu.make_async_copy(f1_ref, f1_full.at[zl, y], own_sem.at[0]),
        pltpu.make_async_copy(f2_ref, f2_full.at[pb], own_sem.at[1]),
    ]
    barrier = pltpu.get_barrier_semaphore()
    peers = [at_x(k) for k in (1, 3)] + [at_y(k) for k in (1, 2, 3)] + [at_zl(k) for k in (1, 2, 3)] + [across]
    for peer in peers:
        pl.semaphore_signal(barrier, inc=1, device_id=peer, device_id_type=MESH)
    for c in own + loads:
        c.start()
    pl.semaphore_wait(barrier, len(peers))

    def ring_first(side, src, part):
        h = 0 if side is None else 1
        base = 2 + 6 * h
        block = f2_full.at[pb if h == 0 else (1 - zh) * 4 + x, halves[part]]
        for way, k in ((0, 1), (1, 3)):
            i = base + way + (0 if part == way else 2)
            start(src, block, f2_send.at[i], f2_recv.at[i], at_x(k))

    def block_of(h, k):
        return (zh if h == 0 else 1 - zh) * 4 + near(k)

    def ring_second(h, way):
        base = 2 + 6 * h
        back, on = ((3, 1), (1, 3))[way]
        got = f2_full.at[block_of(h, back), halves[way]]
        arrived(got, f2_send.at[base + way], f2_recv.at[base + way], at_x(on))
        start(got, got, f2_send.at[base + 4 + way], f2_recv.at[base + 4 + way], at_x(on))

    def ring_rest(h):
        base = 2 + 6 * h
        for way, (back, on) in enumerate(((3, 1), (1, 3))):
            got = f2_full.at[block_of(h, back), halves[1 - way]]
            arrived(got, f2_send.at[base + 2 + way], f2_recv.at[base + 2 + way], at_x(on))
            got = f2_full.at[block_of(h, 2), halves[way]]
            arrived(got, f2_send.at[base + 4 + way], f2_recv.at[base + 4 + way], at_x(on))

    for k in (1, 2, 3):
        start(f1_ref, f1_full.at[zl, y], f1_send.at[k - 1], f1_recv.at[k - 1], at_zl(k))
    for part in (0, 1):
        start(
            f2_ref.at[halves[part]], f2_full.at[pb, halves[part]], f2_send.at[part], f2_recv.at[part], across
        )
    for part in (0, 1):
        ring_first(None, f2_ref.at[halves[part]], part)
    for k in (1, 2, 3):
        start(f1_ref, f1_full.at[zl, y], f1_send.at[2 + k], f1_recv.at[2 + k], at_y(k))

    a3 = spread_matrix(32, 3, 1.0 / 64).astype(BF)
    fine = spread_matrix(128, 1, 0.25).astype(BF)
    coarse = [spread_matrix(128, 2, 1.0 / 16, 64 * j).astype(BF) for j in range(2)]
    both = [jnp.concatenate([fine, coarse[j]], axis=0) for j in range(2)]
    ring_second(0, 0)
    ring_second(0, 1)

    for k in (1, 2, 3):
        got = f1_full.at[(zl + 4 - k) % 4, y]
        arrived(got, f1_send.at[k - 1], f1_recv.at[k - 1], at_zl(k))
        for m in (1, 2, 3):
            i = 3 + 3 * k + m - 1
            start(got, got, f1_send.at[i], f1_recv.at[i], at_y(m))

    for c in own + loads:
        c.wait()

    def merge(i, _):
        rows = pl.ds(pl.multiple_of(i * 256, 256), 256)
        third = mm(c3[:, rows], a3, 0, 0)
        second = c2[rows, :]
        for k in range(4):
            left = jnp.concatenate([c1[rows, k * 128:(k + 1) * 128], second], axis=1)
            upper = mm(left, both[k // 2]) + third
            for r in (2 * k, 2 * k + 1):
                cols = slice(r * W, (r + 1) * W)
                comb[rows, cols] = (comb[rows, cols].astype(F32) + upper).astype(BF)
        return 0

    def other_first(part):
        got = f2_full.at[(1 - zh) * 4 + x, halves[part]]
        arrived(got, f2_send.at[part], f2_recv.at[part], across)
        ring_first(1, got, part)

    steps = nq // 256
    lax.fori_loop(0, steps // 2, merge, 0)
    other_first(0)
    other_first(1)
    lax.fori_loop(steps // 2, steps, merge, 0)

    for k in (1, 2, 3):
        arrived(f1_full.at[zl, (y + 4 - k) % 4], f1_send.at[2 + k], f1_recv.at[2 + k], at_y(k))
        for m in (1, 2, 3):
            i = 3 + 3 * m + k - 1
            arrived(f1_full.at[(zl + 4 - m) % 4, (y + 4 - k) % 4], f1_send.at[i], f1_recv.at[i], at_y(k))
    ring_second(1, 0)
    ring_second(1, 1)

    first = f1_full[...].reshape(C, nq)

    def target(n, _):
        cols = pl.ds(pl.multiple_of(n * W, W), W)
        part = mm(first, comb[:, cols]) * FACTOR
        gt[:, :, :, cols] = part.astype(BF).reshape(2, 4, 32, W)
        return 0

    lax.fori_loop(0, nt // W, target, 0)

    def side_of(h):
        return (1 - zh) if h == 0 else zh

    def scatter_first(h):
        base = 6 * h
        for way, k in ((0, 1), (1, 3)):
            start(
                gt.at[side_of(h), near(2), halves[way]], gt_in.at[h, way],
                gt_send.at[base + way], gt_recv.at[base + way], at_x(k),
            )
        for way, k in ((0, 1), (1, 3)):
            start(
                gt.at[side_of(h), near(k), halves[1 - way]], gt_in.at[h, 2 + way],
                gt_send.at[base + 2 + way], gt_recv.at[base + 2 + way], at_x(k),
            )

    def scatter_second(h):
        base = 6 * h
        for way, k in ((0, 1), (1, 3)):
            arrived(gt_in.at[h, way], gt_send.at[base + way], gt_recv.at[base + way], at_x(k))
            here = gt[side_of(h), near(k), halves[way], :].astype(F32)
            gt_mid[h, way] = (here + gt_in[h, way].astype(F32)).astype(BF)
            start(
                gt_mid.at[h, way], gt_in.at[h, 4 + way],
                gt_send.at[base + 4 + way], gt_recv.at[base + 4 + way], at_x(k),
            )

    def scatter_total(h, part):
        base = 6 * h
        total = gt[side_of(h), x, halves[part], :].astype(F32)
        for way, k in ((0, 1), (1, 3)):
            i = (4 if way == part else 2) + way
            arrived(gt_in.at[h, i], gt_send.at[base + i], gt_recv.at[base + i], at_x(k))
            total = total + gt_in[h, i].astype(F32)
        return total

    scatter_first(0)
    scatter_first(1)

    ring_rest(0)
    ring_rest(1)

    second = f2_full[...].reshape(C, nt)

    def query(n, _):
        rows = pl.ds(pl.multiple_of(n * 256, 256), 256)
        part = mm(second, comb[rows, :], 1, 1) * FACTOR
        gq[:, :, :, rows] = part.astype(BF).reshape(4, 4, 16, 256)
        return 0

    lax.fori_loop(0, nq // 256, query, 0)
    for k in (1, 2, 3):
        start(gq.at[:, (y + k) % 4], gq_in.at[k - 1], gq_send.at[k - 1], gq_recv.at[k - 1], at_y(k))

    scatter_second(0)
    scatter_second(1)

    narrow = [spread_matrix(W // 2 ** l, l, 4.0 ** -l).astype(BF) for l in (1, 2, 3)]
    mean = jnp.concatenate(narrow + [jnp.zeros((32, W), BF)], axis=0)
    images = [mm(second[:, r * W:(r + 1) * W], mean, 1, 1) for r in range(8)]
    pairs = [images[2 * k] + images[2 * k + 1] for k in range(4)]
    fours = [pairs[2 * k] + pairs[2 * k + 1] for k in range(2)]
    eight = fours[0] + fours[1]

    def put(ref, value, cols):
        high = value.astype(BF)
        ref[0, :, cols] = high
        ref[1, :, cols] = (value - high.astype(F32)).astype(BF)

    for k in range(4):
        put(p1, pairs[k][:, :128], slice(k * 128, (k + 1) * 128))
    put(p2, jnp.concatenate([f[:, 128:192] for f in fours], axis=1), slice(0, 128))
    put(p3, eight[:, 192:224], slice(0, 32))

    def volume(n, _):
        rows = pl.ds(pl.multiple_of(n * 256, 256), 256)
        columns = f1_full[:, :, :, rows].reshape(C, 256)
        query = columns.T
        for r in range(8):
            cols = slice(r * W, (r + 1) * W)
            corr0[rows, cols] = (mm(query, f2_full[:, :, cols].reshape(C, W)) * FACTOR).astype(BF)
        corr1[rows, :] = ((mm(query, p1[0]) + mm(query, p1[1])) * FACTOR).astype(BF)
        corr2[rows, :] = ((mm(query, p2[0]) + mm(query, p2[1])) * FACTOR).astype(BF)
        corr3[:, rows] = ((mm(p3[0], columns, 0, 0) + mm(p3[1], columns, 0, 0)) * FACTOR).astype(BF)
        return 0

    lax.fori_loop(0, nq // 256, volume, 0)

    for part in (0, 1):
        gt_out[halves[part], :] = scatter_total(0, part).astype(BF)
        start(
            gt_out.at[halves[part]], gt_in_z.at[halves[part]], gt_send.at[12 + part], gt_recv.at[12 + part], across
        )

    for k in (1, 2, 3):
        arrived(gq_in.at[k - 1], gq_send.at[k - 1], gq_recv.at[k - 1], at_y(k))
    for k in (1, 2, 3, 0):
        to = (zl + k) % 4
        total = gq[to, y].astype(F32)
        for m in range(3):
            total = total + gq_in[m, to].astype(F32)
        if k:
            gq_out[k - 1] = total.astype(BF)
            start(gq_out.at[k - 1], gq_in_z.at[k - 1], gq_send.at[2 + k], gq_recv.at[2 + k], at_zl(k))
        else:
            gq_sum[...] = total
    for part in (0, 1):
        gt_sum[halves[part], :] = scatter_total(1, part)

    for k in (1, 2, 3):
        arrived(gq_in_z.at[k - 1], gq_send.at[2 + k], gq_recv.at[2 + k], at_zl(k))
    for part in (0, 1):
        arrived(gt_in_z.at[halves[part]], gt_send.at[12 + part], gt_recv.at[12 + part], across)
    for c in sent:
        c.wait_send()


def finish(
    v0, v1, v2, v3, gt_sum, gt_in_z, gq_sum, gq_in_z,
    corr0, corr1, corr2, corr3, grad_query, grad_target,
    gq, gt, sem,
):
    copies = [
        pltpu.make_async_copy(src, dst, sem.at[i])
        for i, (src, dst) in enumerate(
            ((v0, corr0), (v1, corr1), (v2, corr2), (v3, corr3), (gq, grad_query), (gt, grad_target))
        )
    ]
    for c in copies[:4]:
        c.start()
    total = gq_sum[...]
    for k in range(3):
        total = total + gq_in_z[k].astype(F32)
    gq[...] = total.astype(BF)
    copies[4].start()
    gt[...] = (gt_sum[...] + gt_in_z[...].astype(F32)).astype(BF)
    copies[5].start()
    for c in copies:
        c.wait()


def body(fmap1, fmap2, cot0, cot1, cot2, cot3):
    nq, nt = cot0.shape
    hbm = pl.BlockSpec(memory_space=pltpu.HBM)
    vmem = pl.BlockSpec(memory_space=pltpu.VMEM)
    dma = pltpu.SemaphoreType.DMA
    sds = jax.ShapeDtypeStruct
    volumes = (sds((nq, nt), BF), sds((nq, nt // 4), BF), sds((nq, nt // 16), BF), sds((nt // 64, nq), BF))
    args = (fmap1.T, fmap2.T, cot0, cot1, cot2, cot3.T)
    parts = pl.pallas_call(
        exchange,
        out_shape=volumes + (
            sds((32, nt), F32),
            sds((32, nt), BF),
            sds((16, nq), F32),
            sds((3, 16, nq), BF),
        ),
        in_specs=[hbm] * 6,
        out_specs=(vmem,) * 8,
        scratch_shapes=[
            pltpu.VMEM((4, 4, 16, nq), BF),
            pltpu.VMEM((8, 32, nt), BF),
            pltpu.VMEM((nq, nt), BF),
            pltpu.VMEM((nq, nt // 4), BF),
            pltpu.VMEM((nq, nt // 16), BF),
            pltpu.VMEM((nt // 64, nq), BF),
            pltpu.VMEM((2, C, nt // 4), BF),
            pltpu.VMEM((2, C, nt // 16), BF),
            pltpu.VMEM((2, C, nt // 64), BF),
            pltpu.VMEM((2, 4, 32, nt), BF),
            pltpu.VMEM((4, 4, 16, nq), BF),
            pltpu.VMEM((2, 6, 16, nt), BF),
            pltpu.VMEM((2, 2, 16, nt), BF),
            pltpu.VMEM((32, nt), BF),
            pltpu.VMEM((3, 4, 16, nq), BF),
            pltpu.VMEM((3, 16, nq), BF),
            dma((4,)),
            dma((2,)),
            dma((15,)),
            dma((15,)),
            dma((14,)),
            dma((14,)),
            dma((14,)),
            dma((14,)),
            dma((6,)),
            dma((6,)),
        ],
        compiler_params=pltpu.CompilerParams(
            collective_id=0, has_side_effects=True, vmem_limit_bytes=40 * 2**20
        ),
        cost_estimate=pl.CostEstimate(flops=10 * nq * nt * C, bytes_accessed=16 * 2**20, transcendentals=0),
        name="exchange",
    )(*(pltpu.with_memory_space_constraint(a, pltpu.HBM) for a in args))
    corr0, corr1, corr2, corr3, grad_query, grad_target = pl.pallas_call(
        finish,
        out_shape=volumes + (sds((16, nq), BF), sds((32, nt), BF)),
        in_specs=[vmem] * 8,
        out_specs=(hbm,) * 6,
        scratch_shapes=[pltpu.VMEM((16, nq), BF), pltpu.VMEM((32, nt), BF), dma((6,))],
        compiler_params=pltpu.CompilerParams(vmem_limit_bytes=16 * 2**20),
        cost_estimate=pl.CostEstimate(flops=0, bytes_accessed=8 * 2**20, transcendentals=0),
        name="finish",
    )(*parts)
    return corr0, corr1, corr2, corr3.T, grad_query.T, grad_target.T


def solution(mesh):
    rows, flat = P(("dp", "pb"), "ta"), P(("dp", "ta"), "pb")
    return jax.shard_map(
        body,
        mesh=mesh,
        in_specs=(rows, flat, rows, rows, rows, rows),
        out_specs=(rows, rows, rows, rows, rows, flat),
        check_vma=False,
    )
```

```python
import functools
import math

import jax
import jax.numpy as jnp
from jax import lax
from jax.experimental import pallas as pl
from jax.experimental.pallas import tpu as pltpu
from jax.sharding import PartitionSpec as P

C = 256
W = 256
MESH = pl.DeviceIdType.MESH
BF = jnp.bfloat16
F32 = jnp.float32
FACTOR = 1.0 / math.sqrt(C)


def mm(a, b, ca=1, cb=0):
    return lax.dot_general(a, b, (((ca,), (cb,)), ((), ())), preferred_element_type=F32)


def spread_matrix(rows, shift, value, offset=0):
    row = lax.broadcasted_iota(jnp.int32, (rows, W), 0) - offset
    col = lax.broadcasted_iota(jnp.int32, (rows, W), 1)
    return jnp.where(row == (col >> shift), value, 0.0)


def exchange(
    f1_ref, f2_ref, cot0_ref, cot1_ref, cot2_ref, cot3_ref,
    corr0, corr1, corr2, corr3, gt_sum, gt_in_z, gq_sum, gq_in_z,
    f1_full, f2_full, comb, c1, c2, c3, p1, p2, p3, gt, gq, gt_in, gt_out, gq_in, gq_out,
    load_sem, own_sem, f1_send, f1_recv, f2_send, f2_recv, gt_send, gt_recv, gq_send, gq_recv,
):
    dp, pb, ta = lax.axis_index("dp"), lax.axis_index("pb"), lax.axis_index("ta")
    zh, x = pb // 4, pb % 4
    zl, y = ta // 4, ta % 4
    nq, nt = comb.shape
    halves = (pl.ds(0, 16), pl.ds(16, 16))

    def near(k):
        return (x + k) % 4

    def at_x(k):
        return (dp, zh * 4 + near(k), ta)

    def at_y(k):
        return (dp, pb, zl * 4 + (y + k) % 4)

    def at_zl(k):
        return (dp, pb, ((zl + k) % 4) * 4 + y)

    across = (dp, (1 - zh) * 4 + x, ta)

    def copy(src, dst, send, recv, to):
        return pltpu.make_async_remote_copy(
            src_ref=src, dst_ref=dst, send_sem=send, recv_sem=recv, device_id=to, device_id_type=MESH
        )

    sent = []

    def start(*args):
        c = copy(*args)
        c.start()
        sent.append(c)

    def arrived(dst, send, recv, to):
        copy(dst, dst, send, recv, to).wait_recv()

    loads = [
        pltpu.make_async_copy(src, dst, load_sem.at[i])
        for i, (src, dst) in enumerate(((cot3_ref, c3), (cot2_ref, c2), (cot1_ref, c1), (cot0_ref, comb)))
    ]
    own = [
        pltpu.make_async_copy(f1_ref, f1_full.at[zl, y], own_sem.at[0]),
        pltpu.make_async_copy(f2_ref, f2_full.at[pb], own_sem.at[1]),
    ]
    barrier = pltpu.get_barrier_semaphore()
    peers = [at_x(k) for k in (1, 2, 3)] + [at_y(k) for k in (1, 2, 3)] + [at_zl(k) for k in (1, 2, 3)] + [across]
    for peer in peers:
        pl.semaphore_signal(barrier, inc=1, device_id=peer, device_id_type=MESH)
    for c in own + loads:
        c.start()
    pl.semaphore_wait(barrier, len(peers))

    def ring_first(part):
        for way, k in ((0, 1), (1, 3)):
            i = way + (0 if part == way else 2)
            start(f2_ref.at[halves[part]], f2_full.at[pb, halves[part]], f2_send.at[i], f2_recv.at[i], at_x(k))

    def ring_second(way):
        back, on = ((3, 1), (1, 3))[way]
        got = f2_full.at[zh * 4 + near(back), halves[way]]
        arrived(got, f2_send.at[way], f2_recv.at[way], at_x(on))
        start(got, got, f2_send.at[4 + way], f2_recv.at[4 + way], at_x(on))

    def ring_rest():
        for way, (back, on) in enumerate(((3, 1), (1, 3))):
            got = f2_full.at[zh * 4 + near(back), halves[1 - way]]
            arrived(got, f2_send.at[2 + way], f2_recv.at[2 + way], at_x(on))
            got = f2_full.at[zh * 4 + near(2), halves[way]]
            arrived(got, f2_send.at[4 + way], f2_recv.at[4 + way], at_x(on))

    pieces = [pl.ds(c * (nt // 4), nt // 4) for c in range(4)]
    piece_copies = [
        copy(
            f2_ref.at[:, pieces[c]], f2_full.at[pb, :, pieces[c]], f2_send.at[6 + c], f2_recv.at[6 + c], across
        )
        for c in range(4)
    ]

    def next_piece(c):
        piece_copies[c - 1].wait_send()
        piece_copies[c].start()

    def pass_piece(c):
        got = f2_full.at[(1 - zh) * 4 + x, :, pieces[c]]
        arrived(got, f2_send.at[6 + c], f2_recv.at[6 + c], across)
        for k in (1, 2, 3):
            i = 9 + 3 * c + k
            start(got, got, f2_send.at[i], f2_recv.at[i], at_x(k))

    def await_pieces():
        for c in range(4):
            for k in (1, 2, 3):
                i = 9 + 3 * c + k
                arrived(f2_full.at[(1 - zh) * 4 + near(4 - k), :, pieces[c]], f2_send.at[i], f2_recv.at[i], at_x(k))

    for k in (1, 2, 3):
        start(f1_ref, f1_full.at[zl, y], f1_send.at[k - 1], f1_recv.at[k - 1], at_zl(k))
    for c in piece_copies:
        c.start()
        sent.append(c)
    for part in (0, 1):
        ring_first(part)
    for k in (1, 2, 3):
        start(f1_ref, f1_full.at[zl, y], f1_send.at[2 + k], f1_recv.at[2 + k], at_y(k))

    a3 = spread_matrix(32, 3, 1.0 / 64).astype(BF)
    fine = spread_matrix(128, 1, 0.25).astype(BF)
    coarse = [spread_matrix(128, 2, 1.0 / 16, 64 * j).astype(BF) for j in range(2)]
    both = [jnp.concatenate([fine, coarse[j]], axis=0) for j in range(2)]
    ring_second(0)
    ring_second(1)

    for k in (1, 2, 3):
        got = f1_full.at[(zl + 4 - k) % 4, y]
        arrived(got, f1_send.at[k - 1], f1_recv.at[k - 1], at_zl(k))
        for m in (1, 2, 3):
            i = 3 + 3 * k + m - 1
            start(got, got, f1_send.at[i], f1_recv.at[i], at_y(m))

    for c in own + loads:
        c.wait()

    def merge(i, _):
        rows = pl.ds(pl.multiple_of(i * 256, 256), 256)
        third = mm(c3[:, rows], a3, 0, 0)
        second = c2[rows, :]
        for k in range(4):
            left = jnp.concatenate([c1[rows, k * 128:(k + 1) * 128], second], axis=1)
            upper = mm(left, both[k // 2]) + third
            for r in (2 * k, 2 * k + 1):
                cols = slice(r * W, (r + 1) * W)
                comb[rows, cols] = (comb[rows, cols].astype(F32) + upper).astype(BF)
        return 0

    steps = nq // 256
    pass_piece(0)
    lax.fori_loop(0, steps // 2, merge, 0)
    pass_piece(1)
    lax.fori_loop(steps // 2, steps, merge, 0)
    pass_piece(2)
    pass_piece(3)

    def query_half(side):
        channels = f2_full[pl.ds(4 * side, 4)].reshape(C // 2, nt)

        def query(n, _):
            rows = pl.ds(pl.multiple_of(n * 256, 256), 256)
            part = mm(channels, comb[rows, :], 1, 1) * FACTOR
            gq[pl.ds(2 * side, 2), :, :, rows] = part.astype(BF).reshape(2, 4, 16, 256)
            return 0

        lax.fori_loop(0, nq // 256, query, 0)

    def query_scatter(p, side):
        for k in (1, 2, 3):
            i = 3 * p + k - 1
            start(gq.at[pl.ds(2 * side, 2), (y + k) % 4], gq_in.at[p, k - 1], gq_send.at[i], gq_recv.at[i], at_y(k))

    late = []

    def query_total(p, side):
        for k in (1, 2, 3):
            i = 3 * p + k - 1
            arrived(gq_in.at[p, k - 1], gq_send.at[i], gq_recv.at[i], at_y(k))
        for j in (0, 1):
            to = 2 * side + j
            k = (to + 4 - zl) % 4
            total = gq[to, y].astype(F32)
            for m in range(3):
                total = total + gq_in[p, m, j].astype(F32)
            gq_out[2 * p + j] = total.astype(BF)
            c = copy(
                gq_out.at[2 * p + j], gq_in_z.at[(k + 3) % 4], gq_send.at[6 + (k + 3) % 4],
                gq_recv.at[6 + (k + 3) % 4], (dp, pb, to * 4 + y),
            )

            @pl.when(to == zl)
            def _():
                gq_sum[...] = total

            pl.when(to != zl)(c.start)
            late.append((to, c))


    for k in (1, 2, 3):
        arrived(f1_full.at[zl, (y + 4 - k) % 4], f1_send.at[2 + k], f1_recv.at[2 + k], at_y(k))
        for m in (1, 2, 3):
            i = 3 + 3 * m + k - 1
            arrived(f1_full.at[(zl + 4 - m) % 4, (y + 4 - k) % 4], f1_send.at[i], f1_recv.at[i], at_y(k))

    first = f1_full[...].reshape(C, nq)

    def target(n, _):
        cols = pl.ds(pl.multiple_of(n * W, W), W)
        part = mm(first, comb[:, cols]) * FACTOR
        gt[:, :, :, cols] = part.astype(BF).reshape(2, 4, 32, W)
        return 0

    lax.fori_loop(0, nt // W, target, 0)

    spans = [(1 - zh, pl.ds(0, nt // 2)), (1 - zh, pl.ds(nt // 2, nt // 2)), (zh, pl.ds(0, nt))]

    def scatter(n):
        side, cols = spans[n]
        for k in (1, 2, 3):
            i = 3 * n + k - 1
            start(
                gt.at[side, near(k), :, cols], gt_in.at[n // 2, k - 1, :, cols],
                gt_send.at[i], gt_recv.at[i], at_x(k),
            )

    def scatter_total(n):
        side, cols = spans[n]
        total = gt[side, x, :, cols].astype(F32)
        for k in (1, 2, 3):
            i = 3 * n + k - 1
            arrived(gt_in.at[n // 2, k - 1, :, cols], gt_send.at[i], gt_recv.at[i], at_x(k))
            total = total + gt_in[n // 2, k - 1, :, cols].astype(F32)
        return total

    def cross(n):
        cols = spans[n][1]
        gt_out[:, cols] = scatter_total(n).astype(BF)
        start(gt_out.at[:, cols], gt_in_z.at[:, cols], gt_send.at[9 + n], gt_recv.at[9 + n], across)

    scatter(0)
    scatter(1)
    ring_rest()
    query_half(zh)
    query_scatter(0, zh)
    await_pieces()
    query_half(1 - zh)
    query_scatter(1, 1 - zh)
    scatter(2)
    query_total(0, zh)
    cross(0)
    cross(1)
    query_total(1, 1 - zh)

    second = f2_full[...].reshape(C, nt)
    narrow = [spread_matrix(W // 2 ** l, l, 4.0 ** -l).astype(BF) for l in (1, 2, 3)]
    mean = jnp.concatenate(narrow + [jnp.zeros((32, W), BF)], axis=0)
    images = [mm(second[:, r * W:(r + 1) * W], mean, 1, 1) for r in range(8)]
    pairs = [images[2 * k] + images[2 * k + 1] for k in range(4)]
    fours = [pairs[2 * k] + pairs[2 * k + 1] for k in range(2)]
    eight = fours[0] + fours[1]

    def put(ref, value, cols):
        high = value.astype(BF)
        ref[0, :, cols] = high
        ref[1, :, cols] = (value - high.astype(F32)).astype(BF)

    for k in range(4):
        put(p1, pairs[k][:, :128], slice(k * 128, (k + 1) * 128))
    put(p2, jnp.concatenate([f[:, 128:192] for f in fours], axis=1), slice(0, 128))
    put(p3, eight[:, 192:224], slice(0, 32))

    def volume(n, _):
        rows = pl.ds(pl.multiple_of(n * 256, 256), 256)
        columns = f1_full[:, :, :, rows].reshape(C, 256)
        query = columns.T
        for r in range(8):
            cols = slice(r * W, (r + 1) * W)
            corr0[rows, cols] = (mm(query, f2_full[:, :, cols].reshape(C, W)) * FACTOR).astype(BF)
        corr1[rows, :] = ((mm(query, p1[0]) + mm(query, p1[1])) * FACTOR).astype(BF)
        corr2[rows, :] = ((mm(query, p2[0]) + mm(query, p2[1])) * FACTOR).astype(BF)
        corr3[:, rows] = ((mm(p3[0], columns, 0, 0) + mm(p3[1], columns, 0, 0)) * FACTOR).astype(BF)
        return 0

    lax.fori_loop(0, nq // 256, volume, 0)

    gt_sum[...] = scatter_total(2)
    for k in (1, 2, 3):
        arrived(gq_in_z.at[k - 1], gq_send.at[5 + k], gq_recv.at[5 + k], at_zl(k))
    for n in (0, 1):
        arrived(gt_in_z.at[:, spans[n][1]], gt_send.at[9 + n], gt_recv.at[9 + n], across)
    for c in sent:
        c.wait_send()
    for to, c in late:
        pl.when(to != zl)(c.wait_send)


def finish(
    v0, v1, v2, v3, gt_sum, gt_in_z, gq_sum, gq_in_z,
    corr0, corr1, corr2, corr3, grad_query, grad_target,
    gq, gt, sem,
):
    copies = [
        pltpu.make_async_copy(src, dst, sem.at[i])
        for i, (src, dst) in enumerate(
            ((v0, corr0), (v1, corr1), (v2, corr2), (v3, corr3), (gq, grad_query), (gt, grad_target))
        )
    ]
    for c in copies[:4]:
        c.start()
    total = gq_sum[...]
    for k in range(3):
        total = total + gq_in_z[k].astype(F32)
    gq[...] = total.astype(BF)
    copies[4].start()
    gt[...] = (gt_sum[...] + gt_in_z[...].astype(F32)).astype(BF)
    copies[5].start()
    for c in copies:
        c.wait()


def body(fmap1, fmap2, cot0, cot1, cot2, cot3):
    nq, nt = cot0.shape
    hbm = pl.BlockSpec(memory_space=pltpu.HBM)
    vmem = pl.BlockSpec(memory_space=pltpu.VMEM)
    dma = pltpu.SemaphoreType.DMA
    sds = jax.ShapeDtypeStruct
    volumes = (sds((nq, nt), BF), sds((nq, nt // 4), BF), sds((nq, nt // 16), BF), sds((nt // 64, nq), BF))
    args = (fmap1.T, fmap2.T, cot0, cot1, cot2, cot3.T)
    parts = pl.pallas_call(
        exchange,
        out_shape=volumes + (
            sds((32, nt), F32),
            sds((32, nt), BF),
            sds((16, nq), F32),
            sds((3, 16, nq), BF),
        ),
        in_specs=[hbm] * 6,
        out_specs=(vmem,) * 8,
        scratch_shapes=[
            pltpu.VMEM((4, 4, 16, nq), BF),
            pltpu.VMEM((8, 32, nt), BF),
            pltpu.VMEM((nq, nt), BF),
            pltpu.VMEM((nq, nt // 4), BF),
            pltpu.VMEM((nq, nt // 16), BF),
            pltpu.VMEM((nt // 64, nq), BF),
            pltpu.VMEM((2, C, nt // 4), BF),
            pltpu.VMEM((2, C, nt // 16), BF),
            pltpu.VMEM((2, C, nt // 64), BF),
            pltpu.VMEM((2, 4, 32, nt), BF),
            pltpu.VMEM((4, 4, 16, nq), BF),
            pltpu.VMEM((2, 3, 32, nt), BF),
            pltpu.VMEM((32, nt), BF),
            pltpu.VMEM((2, 3, 2, 16, nq), BF),
            pltpu.VMEM((4, 16, nq), BF),
            dma((4,)),
            dma((2,)),
            dma((15,)),
            dma((15,)),
            dma((22,)),
            dma((22,)),
            dma((11,)),
            dma((11,)),
            dma((9,)),
            dma((9,)),
        ],
        compiler_params=pltpu.CompilerParams(
            collective_id=0, has_side_effects=True, vmem_limit_bytes=40 * 2**20
        ),
        cost_estimate=pl.CostEstimate(flops=10 * nq * nt * C, bytes_accessed=16 * 2**20, transcendentals=0),
        name="exchange",
    )(*(pltpu.with_memory_space_constraint(a, pltpu.HBM) for a in args))
    corr0, corr1, corr2, corr3, grad_query, grad_target = pl.pallas_call(
        finish,
        out_shape=volumes + (sds((16, nq), BF), sds((32, nt), BF)),
        in_specs=[vmem] * 8,
        out_specs=(hbm,) * 6,
        scratch_shapes=[pltpu.VMEM((16, nq), BF), pltpu.VMEM((32, nt), BF), dma((6,))],
        compiler_params=pltpu.CompilerParams(vmem_limit_bytes=16 * 2**20),
        cost_estimate=pl.CostEstimate(flops=0, bytes_accessed=8 * 2**20, transcendentals=0),
        name="finish",
    )(*parts)
    return corr0, corr1, corr2, corr3.T, grad_query.T, grad_target.T


def solution(mesh):
    rows, flat = P(("dp", "pb"), "ta"), P(("dp", "ta"), "pb")
    return jax.shard_map(
        body,
        mesh=mesh,
        in_specs=(rows, flat, rows, rows, rows, rows),
        out_specs=(rows, rows, rows, rows, rows, flat),
        check_vma=False,
    )
```
